256 devices in a mesh: cfg: 2 (over core), uly: 4 (over y), blk: 32 (over x, z).
Axes of the slice: x: 4, y: 4, z: 8, core: 2. Of those that a mesh axis runs over, the one named last changes fastest.
Arguments:
- residual_in: bfloat16 [2, 8192, 5120], P('cfg', ('uly', 'blk')), may hold values from -1.1953125 to 1.1953125
- projected: bfloat16 [2, 8192, 7680], P('cfg', ('uly', 'blk')), may hold values from -1500 to 1500, as said below
- query_gain: float32 [2560], replicated, may hold values from 0.6 to 5
- key_gain: float32 [2560], replicated, may hold values from 0.6 to 5
- gate_scale: float32 [5120], replicated, may hold values from -3 to 3
- out_weight: bfloat16 [2560, 5120], P('uly'), may hold values from -0.125 to 0.125
- out_bias: float32 [5120], replicated, may hold values from -3 to 3
Outputs:
- pass_outputs: bfloat16 [2, 8192, 5120], P(None, ('uly', 'blk'), 'cfg')
The draws below stay inside these ranges and needn't reach their ends.
Inputs may be any that keep to these rules, and one draw needn't show every extreme that they name: `projected`: query and key features carry token scales and feature scales; value features are of order one.
All inputs are finite; a program needn't handle non-finite values.
Results may differ from the reference program's by a relative error of at most 0.015.
Values may be sent and summed in bfloat16 or wider, within the bound.
No kernel may reach another device: no remote copies, remote signals or barrier semaphores. Data moves between devices by JAX's collectives and lax.ppermute only.
A program may use at most 192 MiB of HBM per device.

```python
import math
import jax
import jax.numpy as jnp
from jax import lax

D = 5120
HEADS = 20
HEAD = 128
GH = 30
GW = 52
TOKENS = 8192


def scaled_law(key, lower, upper, extent):
    return jnp.exp(jax.random.uniform(key, extent, jnp.float32, math.log(lower), math.log(upper)))


def draw_projected(key, part):
    key = jax.random.fold_in(key, 11)
    subkeys = jax.random.split(key, 9)
    feature_width = HEADS * HEAD
    noise_base = jax.random.truncated_normal(subkeys[0], -4.0, 4.0, (2, TOKENS, 3, feature_width), jnp.float32)
    token_scale = scaled_law(subkeys[1], 1.0, 10.0, (2, TOKENS, 1, 1))
    rising = 3.0 ** (jnp.arange(feature_width, dtype=jnp.float32) / feature_width)
    column_scale = scaled_law(subkeys[2], 1.0, 10.0, (feature_width,)) * rising
    pattern = 2.0 * jax.random.bernoulli(subkeys[7], 0.5, (HEADS, HEAD)).astype(jnp.float32) - 1.0
    common = jax.random.truncated_normal(subkeys[8], -3.0, 3.0, (2, TOKENS, 2, HEADS, 1), jnp.float32)
    shared = (9.0 * common * pattern[None, None, None, :, :]).reshape(2, TOKENS, 2, feature_width)
    query_key = (noise_base[:, :, 0:2] * column_scale + shared) * token_scale
    values = jnp.concatenate([query_key, noise_base[:, :, 2:3]], axis=2)
    return values.reshape(2, TOKENS, 3 * feature_width).astype(jnp.bfloat16)


def draw_query_gain(key, part):
    key = jax.random.fold_in(key, 21)
    return scaled_law(key, 0.6, 1.6, (HEADS * HEAD,))


def draw_key_gain(key, part):
    key = jax.random.fold_in(key, 31)
    return scaled_law(key, 0.6, 1.6, (HEADS * HEAD,))


def levels(stream_key, shape, pieces, smallest, top_value):
    factor_of, own = 1.0, jax.random.fold_in(stream_key, 6)
    for position, blocks in pieces:
        draws = jnp.exp(jax.random.uniform(jax.random.fold_in(own, position), (blocks,), jnp.float32, smallest / len(pieces), top_value / len(pieces)))
        factor_of = factor_of * jnp.repeat(draws, shape[position] // blocks).reshape([-1 if axis == position else 1 for axis in range(len(shape))])
    return factor_of


def noise(key, shape, scale, reach, pieces=(), kind=jnp.bfloat16):
    level = levels(key, shape, pieces, -0.22, 0.18) if pieces else 1.0
    drawn = jax.random.normal(key, shape, jnp.float32) * scale * level
    return jnp.minimum(jnp.maximum(drawn, -reach), reach).astype(kind)


def setup_inputs(seed: int = 0) -> dict:
    arg_keys = jax.random.split(jax.random.key(seed), 8)
    residual_in = noise(arg_keys[0], (2, TOKENS, D), 0.2, 1.1953125, ((0, 2), (1, 128)))
    projected = draw_projected(jax.random.fold_in(arg_keys[7], 71), 0)
    query_gain = draw_query_gain(jax.random.fold_in(arg_keys[7], 71), 0)
    key_gain = draw_key_gain(jax.random.fold_in(arg_keys[7], 71), 0)
    gate_scale = noise(arg_keys[4], (D,), 0.5, 3.0, (), jnp.float32)
    out_weight = noise(arg_keys[5], (HEADS * HEAD, D), (HEADS * HEAD) ** -0.5, 0.125, ((0, 4),))
    out_bias = noise(arg_keys[6], (D,), 0.5, 3.0, (), jnp.float32)
    return {"residual_in": residual_in, "projected": projected, "query_gain": query_gain, "key_gain": key_gain, "gate_scale": gate_scale, "out_weight": out_weight, "out_bias": out_bias}


def frequencies(extent):
    return 1.0 / 10000.0 ** (jnp.arange(0, extent, 2, dtype=jnp.float32) / extent)

def rope_angles(positions):
    frame_dims = HEAD - 4 * (HEAD // 6)
    space_dims = 2 * (HEAD // 6)
    frames = (positions // (GH * GW)).astype(jnp.float32)
    height = (positions // GW % GH).astype(jnp.float32)
    across = (positions % GW).astype(jnp.float32)
    return jnp.concatenate([frames[:, None] * frequencies(frame_dims)[None, :], height[:, None] * frequencies(space_dims)[None, :], across[:, None] * frequencies(space_dims)[None, :]], axis=1)

def rotate(values, angles):
    paired = values.reshape(values.shape[0], values.shape[1], HEAD // 2, 2)
    first_half = paired[..., 0]
    second_half = paired[..., 1]
    cosine = jnp.cos(angles)[:, None, :]
    sine = jnp.sin(angles)[:, None, :]
    turned = jnp.stack([first_half * cosine - second_half * sine, first_half * sine + second_half * cosine], axis=-1)
    return turned.reshape(values.shape)

def normalize(values, gain):
    return values * lax.rsqrt(lax.optimization_barrier(jnp.mean(values * values, axis=-1, keepdims=True)) + 1e-06) * gain

def attend_head(inputs):
    queries, keyset, valueset = inputs
    scores = jnp.dot(queries, keyset.T, preferred_element_type=jnp.float32) * HEAD ** (-0.5)
    highest = lax.optimization_barrier(jnp.max(scores, axis=1, keepdims=True))
    expo = jnp.exp(scores - highest)
    totals = lax.optimization_barrier(jnp.sum(expo, axis=1, keepdims=True))
    weights = expo.astype(jnp.bfloat16)
    return (jnp.dot(weights, valueset, preferred_element_type=jnp.float32) / totals).astype(jnp.bfloat16)

def reference(residual_in, projected, query_gain, key_gain, gate_scale, out_weight, out_bias):
    positions = jnp.arange(TOKENS, dtype=jnp.int32)
    angles = rope_angles(positions)
    feature_width = HEADS * HEAD
    outputs = []
    for branch in range(2):
        layers = projected[branch].reshape(TOKENS, 3, feature_width)
        queries = rotate(normalize(layers[:, 0].astype(jnp.float32), query_gain).reshape(TOKENS, HEADS, HEAD), angles).astype(jnp.bfloat16)
        keyset = rotate(normalize(layers[:, 1].astype(jnp.float32), key_gain).reshape(TOKENS, HEADS, HEAD), angles).astype(jnp.bfloat16)
        valueset = layers[:, 2].reshape(TOKENS, HEADS, HEAD)
        heads_out = lax.map(attend_head, (queries.transpose(1, 0, 2), keyset.transpose(1, 0, 2), valueset.transpose(1, 0, 2)))
        flat_out = heads_out.transpose(1, 0, 2).reshape(TOKENS, feature_width)
        mixed = jnp.dot(flat_out, out_weight, preferred_element_type=jnp.float32)
        outputs.append(residual_in[branch].astype(jnp.float32) + gate_scale * (mixed + out_bias))
    return jnp.stack(outputs, axis=0).astype(jnp.bfloat16)
```

```python
import math

import jax
import jax.numpy as jnp
import numpy as np
from jax import lax
from jax.experimental import pallas as pl
from jax.experimental.pallas import tpu as pltpu
from jax.sharding import PartitionSpec as P

D = 5120
HEADS = 20
HEAD = 128
GH = 30
GW = 52
ULY = 4
XS = 4
ZS = 8
ROWS = 64
GROUP = 5
GF = GROUP * HEAD
FEAT = HEADS * HEAD
HALF = D // 2
QUART = HALF // 2
OW = GF + HEAD
BF = jnp.bfloat16
F32 = jnp.float32
SCALE = math.log2(math.e) / math.sqrt(HEAD)
VMEM = 48 * 1024 * 1024


def params():
    return pltpu.CompilerParams(vmem_limit_bytes=VMEM)


def shift_uly(a, s):
    return lax.ppermute(a, "uly", [(i, (i + s) % ULY) for i in range(ULY)])


def shift_x(a, s):
    return lax.ppermute(
        a, "blk", [(x * ZS + z, (x + s) % XS * ZS + z) for x in range(XS) for z in range(ZS)]
    )


def shift_z(a, s):
    return lax.ppermute(
        a, "blk", [(x * ZS + z, x * ZS + (z + s) % ZS) for x in range(XS) for z in range(ZS)]
    )


def swap_cfg(a):
    return lax.ppermute(a, "cfg", [(0, 1), (1, 0)])


def tables(first):
    frame = HEAD - 4 * (HEAD // 6)
    space = 2 * (HEAD // 6)

    def freq(extent):
        return 1.0 / 10000.0 ** (np.arange(0, extent, 2, dtype=np.float32) / np.float32(extent))

    rates = np.repeat(
        np.concatenate([freq(frame), freq(space), freq(space)]).astype(np.float32), 2
    )
    pos = first + lax.broadcasted_iota(jnp.int32, (ROWS, HEAD), 0)
    lane = lax.broadcasted_iota(jnp.int32, (ROWS, HEAD), 1)
    where = jnp.where(
        lane < frame, pos // (GH * GW), jnp.where(lane < frame + space, pos // GW % GH, pos % GW)
    ).astype(F32)
    angle = where * rates[None, :]
    cosine = jnp.cos(angle)
    sine = jnp.sin(angle)
    even = lane % 2 == 0
    return jnp.stack([cosine, jnp.where(even, -sine, 0.0), jnp.where(even, 0.0, sine)])


def prep_body(u_ref, proj_ref, qg_ref, kg_ref, tab_ref, *outs):
    kv_outs, q_outs = outs[:ULY], outs[ULY:]
    u = u_ref[0]
    cosine, s_even, s_odd = tab_ref[0], tab_ref[1], tab_ref[2]

    def scale_of(base):
        total = jnp.zeros((ROWS, HEAD), F32)
        for h in range(HEADS):
            part = proj_ref[0, :, base + h * HEAD : base + (h + 1) * HEAD].astype(F32)
            total = total + part * part
        return lax.rsqrt(jnp.sum(total, axis=1, keepdims=True) * (1.0 / FEAT) + 1e-06)

    q_scale = scale_of(0)
    k_scale = scale_of(FEAT)
    for s in range(ULY):
        start = (u + s) % ULY * GF
        for h in range(GROUP):
            here = slice(h * HEAD, (h + 1) * HEAD)
            for base, scale, gain_ref, out in (
                (0, q_scale, qg_ref, q_outs[s]),
                (FEAT, k_scale, kg_ref, kv_outs[s]),
            ):
                at = pl.multiple_of(start + h * HEAD, HEAD)
                x = proj_ref[0, :, pl.ds(pl.multiple_of(base + at, HEAD), HEAD)].astype(F32)
                x = x * scale * gain_ref[:, pl.ds(at, HEAD)]
                turned = (
                    x * cosine
                    + pltpu.roll(x, HEAD - 1, 1) * s_even
                    + pltpu.roll(x, 1, 1) * s_odd
                )
                out[0:ROWS, here] = turned.astype(BF)
        kv_outs[s][ROWS : 2 * ROWS, :] = proj_ref[
            0, :, pl.ds(pl.multiple_of(2 * FEAT + start, HEAD), GF)
        ]


def prep(u, projected, query_gain, key_gain, tab):
    full = pl.BlockSpec(memory_space=pltpu.VMEM)
    return pl.pallas_call(
        prep_body,
        in_specs=[pl.BlockSpec(memory_space=pltpu.SMEM)] + [full] * 4,
        out_specs=[full] * (2 * ULY),
        out_shape=[jax.ShapeDtypeStruct((2 * ROWS, GF), BF)] * ULY
        + [jax.ShapeDtypeStruct((ROWS, GF), BF)] * ULY,
        compiler_params=params(),
        name="prep",
    )(u, projected, query_gain[None], key_gain[None], tab)


QB = 256


def attend_body(n_kv, first, last, *refs):
    q_ref = refs[0]
    kv_refs = refs[1 : 1 + n_kv]
    rest = refs[1 + n_kv :]
    if not first:
        acc_in, ml_in = rest[:2]
        rest = rest[2:]
    if last:
        (out_ref,) = rest
    else:
        acc_out, ml_out = rest
    lane = lax.broadcasted_iota(jnp.int32, (QB, HEAD), 1)
    stats = jnp.zeros((QB, HEAD), F32)
    for h in range(GROUP):
        here = slice(h * HEAD, (h + 1) * HEAD)
        keys = []
        vals = []
        for ref in kv_refs:
            for b in range(ref.shape[0] // (2 * ROWS)):
                at = b * 2 * ROWS
                keys.append(ref[at : at + ROWS, here])
                vals.append(ref[at + ROWS : at + 2 * ROWS, here])
        keys = jnp.concatenate(keys, axis=0)
        vals = jnp.concatenate(vals, axis=0)
        s = lax.dot_general(
            q_ref[:, here], keys, (((1,), (1,)), ((), ())), preferred_element_type=F32
        )
        m = jnp.max(s, axis=1, keepdims=True) * SCALE
        if not first:
            m_old = ml_in[:, h : h + 1]
            m = jnp.maximum(m, m_old)
        e = jnp.exp2(s * SCALE - m)
        l = jnp.sum(e, axis=1, keepdims=True)
        o = jnp.dot(e.astype(BF), vals, preferred_element_type=F32)
        if not first:
            alpha = jnp.exp2(m_old - m)
            l = l + alpha * ml_in[:, 8 + h : 9 + h]
            o = o + alpha * acc_in[:, here]
        if last:
            out_ref[:, here] = (o / l).astype(BF)
            lse = m + jnp.log2(l)
            hi = lse.astype(BF).astype(F32)
            mid = (lse - hi).astype(BF).astype(F32)
            low = lse - hi - mid
            stats = jnp.where(lane == h, hi, stats)
            stats = jnp.where(lane == 8 + h, mid, stats)
            stats = jnp.where(lane == 16 + h, low, stats)
        else:
            acc_out[:, here] = o
            stats = jnp.where(lane == h, m, stats)
            stats = jnp.where(lane == 8 + h, l, stats)
    if last:
        out_ref[:, GF:] = stats.astype(BF)
    else:
        ml_out[...] = stats


def attend(q, kvs, state=None):
    rows = q.shape[0]

    def row(i):
        return (i, 0)

    specs = [pl.BlockSpec((QB, GF), row)]
    specs += [pl.BlockSpec(kv.shape, lambda i: (0, 0)) for kv in kvs]
    args = [q, *kvs]
    acc_spec = pl.BlockSpec((QB, GF), row)
    ml_spec = pl.BlockSpec((QB, HEAD), row)
    aliases = {}
    if state is not None:
        aliases = {len(args): 0, len(args) + 1: 1}
        specs += [acc_spec, ml_spec]
        args += list(state)
    return pl.pallas_call(
        lambda *r: attend_body(len(kvs), state is None, False, *r),
        grid=(rows // QB,),
        in_specs=specs,
        out_specs=[acc_spec, ml_spec],
        out_shape=[
            jax.ShapeDtypeStruct((rows, GF), F32),
            jax.ShapeDtypeStruct((rows, HEAD), F32),
        ],
        input_output_aliases=aliases,
        compiler_params=params(),
        name="attend",
    )(*args)


def attend_last(q, kvs, state, j):
    def pick(_):
        return (j, 0)

    specs = [pl.BlockSpec((QB, GF), pick)]
    specs += [pl.BlockSpec(kv.shape, lambda i: (0, 0)) for kv in kvs]
    specs += [pl.BlockSpec((QB, GF), pick), pl.BlockSpec((QB, HEAD), pick)]
    return pl.pallas_call(
        lambda *r: attend_body(len(kvs), False, True, *r),
        grid=(1,),
        in_specs=specs,
        out_specs=pl.BlockSpec((QB, OW), lambda i: (0, 0)),
        out_shape=jax.ShapeDtypeStruct((QB, OW), BF),
        compiler_params=params(),
        name="attend_last",
    )(q, *kvs, *state)


def join_body(*refs):
    parts, out_ref = refs[:-1], refs[-1]
    tails = [p[:, GF:].astype(F32) for p in parts]
    for h in range(GROUP):
        here = slice(h * HEAD, (h + 1) * HEAD)
        lse = [t[:, h : h + 1] + t[:, 8 + h : 9 + h] + t[:, 16 + h : 17 + h] for t in tails]
        top = lse[0]
        for other in lse[1:]:
            top = jnp.maximum(top, other)
        weights = [jnp.exp2(v - top) for v in lse]
        total = weights[0]
        for other in weights[1:]:
            total = total + other
        o = weights[0] * parts[0][:, here].astype(F32)
        for w, p in zip(weights[1:], parts[1:]):
            o = o + w * p[:, here].astype(F32)
        out_ref[:, here] = (o / total).astype(BF)


def join(parts):
    full = pl.BlockSpec(memory_space=pltpu.VMEM)
    return pl.pallas_call(
        join_body,
        in_specs=[full] * len(parts),
        out_specs=full,
        out_shape=jax.ShapeDtypeStruct((QB, GF), BF),
        compiler_params=params(),
        name="join",
    )(*parts)


TILE = 640


def project_body(blocks, c_ref, own_ref, other_ref, w_ref, *outs):
    step = pl.program_id(0)
    lhs = jnp.concatenate(
        [ref[b * ROWS : (b + 1) * ROWS, :] for b in blocks for ref in (own_ref, other_ref)], axis=0
    )
    y = jnp.dot(lhs, w_ref[...], preferred_element_type=F32).astype(BF)
    for i in range(len(blocks)):
        part = y[i * 2 * ROWS : (i + 1) * 2 * ROWS]

        @pl.when(step < 2)
        def _(part=part, i=i):
            outs[2 * i][...] = part

        @pl.when(step >= 2)
        def _(part=part, i=i):
            outs[2 * i + 1][...] = part


def project(c, own, other, weight, blocks):
    grid_spec = pltpu.PrefetchScalarGridSpec(
        num_scalar_prefetch=1,
        grid=(HALF // TILE,),
        in_specs=[
            pl.BlockSpec((QB, GF), lambda i, c_ref: (0, 0)),
            pl.BlockSpec((QB, GF), lambda i, c_ref: (0, 0)),
            pl.BlockSpec((GF, TILE), lambda i, c_ref: (0, c_ref[0] * (HALF // TILE) + i)),
        ],
        out_specs=[
            pl.BlockSpec((2 * ROWS, TILE), lambda i, c_ref: (0, jnp.minimum(i, 1))),
            pl.BlockSpec((2 * ROWS, TILE), lambda i, c_ref: (0, jnp.maximum(i - 2, 0))),
        ]
        * len(blocks),
    )
    return pl.pallas_call(
        lambda *r: project_body(blocks, *r),
        grid_spec=grid_spec,
        out_shape=[jax.ShapeDtypeStruct((2 * ROWS, QUART), BF)] * (2 * len(blocks)),
        compiler_params=params(),
        name="project",
    )(c, own, other, weight)


def finish_body(c_ref, own_ref, other_ref, gate_ref, bias_ref, *refs):
    out_ref = refs[-1]
    c = c_ref[0]
    for half in range(2):
        cols = slice(half * QUART, (half + 1) * QUART)
        mixed = refs[half][...].astype(F32)
        for ref in refs[2 + half : 6 : 2]:
            mixed = mixed + ref[...].astype(F32)
        branch = gate_ref[:, cols] * (mixed + bias_ref[:, cols])
        out_ref[c, :, cols] = (own_ref[0, :, cols].astype(F32) + branch[0:ROWS]).astype(BF)
        out_ref[1 - c, :, cols] = (other_ref[:, cols].astype(F32) + branch[ROWS:]).astype(BF)


def finish(c, residual, other, gate, bias, parts):
    piece = pl.BlockSpec((2 * ROWS, QUART), lambda i, c_ref: (0, 0))
    grid_spec = pltpu.PrefetchScalarGridSpec(
        num_scalar_prefetch=1,
        grid=(1,),
        in_specs=[
            pl.BlockSpec((1, ROWS, HALF), lambda i, c_ref: (0, 0, c_ref[0])),
            pl.BlockSpec((ROWS, HALF), lambda i, c_ref: (0, 0)),
            pl.BlockSpec((1, HALF), lambda i, c_ref: (0, c_ref[0])),
            pl.BlockSpec((1, HALF), lambda i, c_ref: (0, c_ref[0])),
        ]
        + [piece] * 6,
        out_specs=pl.BlockSpec((2, ROWS, HALF), lambda i, c_ref: (0, 0, 0)),
    )
    return pl.pallas_call(
        finish_body,
        grid_spec=grid_spec,
        out_shape=jax.ShapeDtypeStruct((2, ROWS, HALF), BF),
        compiler_params=params(),
        name="finish",
    )(c, residual, other, gate[None], bias[None], *parts)


def add(a, b):
    return (a.astype(F32) + b.astype(F32)).astype(BF)


def on_device(residual_in, projected, query_gain, key_gain, gate_scale, out_weight, out_bias):
    u = lax.axis_index("uly")
    b = lax.axis_index("blk")
    c = lax.axis_index("cfg")
    u_arr = u.astype(jnp.int32)[None]
    c_arr = c.astype(jnp.int32)[None]
    tab = tables((u * (XS * ZS) + b) * ROWS)
    outs = prep(u_arr, projected, query_gain, key_gain, tab)
    kv, q = outs[:ULY], outs[ULY:]

    kv1 = shift_uly(kv[1], 1)
    kv3 = shift_uly(kv[3], 3)
    near = jnp.concatenate([kv[0], kv1], axis=0)
    q1 = shift_uly(q[1], 1)
    q3 = shift_uly(q[3], 3)
    kv2 = shift_uly(kv[2], 2)
    q2 = shift_uly(q[2], 2)
    far = jnp.concatenate([kv2, kv3], axis=0)
    q_own = jnp.concatenate([q[0], q1, q2, q3], axis=0)

    q_all = jnp.concatenate([q_own, shift_x(q_own, 1), shift_x(q_own, 2), shift_x(q_own, 3)], axis=0)

    state = attend(q_all, [near, far])
    up = [near, far]
    down = [near, far]
    for _ in range(3):
        up = [shift_z(a, 1) for a in up]
        down = [shift_z(a, -1) for a in down]
        state = attend(q_all, up + down, state)
    kvs = [shift_z(up[0], 1), shift_z(down[1], -1)]

    parts = {}
    for j in (2, 1, 3, 0):
        part = attend_last(q_all, kvs, state, j)
        parts[j] = shift_x(part, -j) if j else part
    mine = join([parts[0], parts[1], parts[2], parts[3]])
    theirs = swap_cfg(mine)

    residual_sent = lax.dynamic_slice(
        residual_in, (0, 0, (1 - c) * HALF), (1, ROWS, HALF)
    )[0]
    residual_other = swap_cfg(residual_sent)

    far_a, far_b = project(c_arr, mine, theirs, out_weight, (2,))
    via_low = shift_uly(far_a, 1)
    via_high = shift_uly(far_b, -1)
    p1a, p1b, p3a, p3b, p0a, p0b = project(c_arr, mine, theirs, out_weight, (1, 3, 0))
    low_b = shift_uly(p3b, 1)
    high_a = shift_uly(p1a, -1)
    low_a = shift_uly(add(p3a, via_low), 1)
    high_b = shift_uly(add(p1b, via_high), -1)
    return finish(
        c_arr,
        residual_in,
        residual_other,
        gate_scale,
        out_bias,
        [p0a, p0b, low_a, low_b, high_a, high_b],
    )


def solution(mesh):
    in_specs = (
        P("cfg", ("uly", "blk"), None),
        P("cfg", ("uly", "blk"), None),
        P(),
        P(),
        P(),
        P("uly", None),
        P(),
    )
    out_specs = P(None, ("uly", "blk"), "cfg")
    return jax.shard_map(
        on_device, mesh=mesh, in_specs=in_specs, out_specs=out_specs, check_vma=False
    )
```

```python
import math

import jax
import jax.numpy as jnp
import numpy as np
from jax import lax
from jax.experimental import pallas as pl
from jax.experimental.pallas import tpu as pltpu
from jax.sharding import Mesh
from jax.sharding import PartitionSpec as P

D = 5120
HEADS = 20
HEAD = 128
GH = 30
GW = 52
ULY = 4
XS = 4
ZS = 8
ROWS = 64
GROUP = 5
GF = GROUP * HEAD
FEAT = HEADS * HEAD
HALF = D // 2
QUART = HALF // 2
OH = GF + 16
BF = jnp.bfloat16
F32 = jnp.float32
SCALE = math.log2(math.e) / math.sqrt(HEAD)
VMEM = 48 * 1024 * 1024


def params(limit=VMEM):
    return pltpu.CompilerParams(vmem_limit_bytes=limit)


def swap_uly(a, s):
    return lax.ppermute(a, "uly", [(i, i ^ s) for i in range(ULY)])


def swap_x(a, s):
    return lax.ppermute(a, "x", [(i, i ^ s) for i in range(XS)])


def swap_z(a, odd):
    return lax.ppermute(a, "z", [(i, ((i - odd ^ 1) + odd) % ZS) for i in range(ZS)])


def swap_cfg(a):
    return lax.ppermute(a, "cfg", [(0, 1), (1, 0)])


FRAME = HEAD - 4 * (HEAD // 6)
SPACE = 2 * (HEAD // 6)


def rates():
    def freq(extent):
        return 1.0 / 10000.0 ** (np.arange(0, extent, 2, dtype=np.float32) / np.float32(extent))

    each = np.concatenate([freq(FRAME), freq(SPACE), freq(SPACE)]).astype(np.float32)
    return np.repeat(each, 2)[None]


def tables(first, rate):
    pos = first + lax.broadcasted_iota(jnp.int32, (ROWS, HEAD), 0)
    lane = lax.broadcasted_iota(jnp.int32, (ROWS, HEAD), 1)
    where = jnp.where(
        lane < FRAME, pos // (GH * GW), jnp.where(lane < FRAME + SPACE, pos // GW % GH, pos % GW)
    ).astype(F32)
    angle = where * rate
    sine = jnp.sin(angle)
    even = lane % 2 == 0
    return jnp.cos(angle), jnp.where(even, -sine, 0.0), jnp.where(even, 0.0, sine)


BLOCK = 3 * ROWS


def prep_body(at_ref, proj_ref, q_gain, k_gain, rate_ref, *outs):
    u = at_ref[0]
    cosine, s_even, s_odd = tables(at_ref[1], rate_ref[...])
    gains = (q_gain, k_gain)

    def scale_of(base):
        total = jnp.zeros((ROWS, HEAD), F32)
        for h in range(HEADS):
            part = proj_ref[0, :, base + h * HEAD : base + (h + 1) * HEAD].astype(F32)
            total = total + part * part
        return lax.rsqrt(jnp.sum(total, axis=1, keepdims=True) * (1.0 / FEAT) + 1e-06)

    scales = (scale_of(0), scale_of(FEAT))

    def turned(which, at):
        x = proj_ref[0, :, pl.ds(pl.multiple_of(which * FEAT + at, HEAD), HEAD)].astype(F32)
        x = x * scales[which] * gains[which][pl.ds(at, HEAD)][None]
        x = x * cosine + pltpu.roll(x, HEAD - 1, 1) * s_even + pltpu.roll(x, 1, 1) * s_odd
        return x.astype(BF)

    for s in range(ULY):
        start = (u ^ s) * GF
        for h in range(GROUP):
            here = slice(h * HEAD, (h + 1) * HEAD)
            at = pl.multiple_of(start + h * HEAD, HEAD)
            outs[s][0:ROWS, here] = turned(1, at)
            outs[s][2 * ROWS :, here] = turned(0, at)
        outs[s][ROWS : 2 * ROWS, :] = proj_ref[
            0, :, pl.ds(pl.multiple_of(2 * FEAT + start, HEAD), GF)
        ]


def prep(place, projected, query_gain, key_gain):
    def whole(shape):
        return pl.BlockSpec(shape, lambda i: (0,) * len(shape))

    rate = jnp.asarray(rates())
    args = (projected, query_gain, key_gain, rate)
    return pl.pallas_call(
        prep_body,
        grid=(1,),
        in_specs=[pl.BlockSpec(memory_space=pltpu.SMEM)] + [whole(a.shape) for a in args],
        out_specs=[whole((BLOCK, GF))] * ULY,
        out_shape=[jax.ShapeDtypeStruct((BLOCK, GF), BF)] * ULY,
        compiler_params=params(62 * 1024 * 1024),
        name="prep",
    )(place, *args)


QB = 256


def heads_step(q, kvs, h, m_old):
    here = slice(h * HEAD, (h + 1) * HEAD)
    keys = jnp.concatenate([kv[0 : kv.shape[0] // 2, here] for kv in kvs], axis=0)
    vals = jnp.concatenate([kv[kv.shape[0] // 2 :, here] for kv in kvs], axis=0)
    s = lax.dot_general(keys, q[:, here], (((1,), (1,)), ((), ())), preferred_element_type=F32)
    m = jnp.max(s, axis=0, keepdims=True) * SCALE
    if m_old is not None:
        m = jnp.maximum(m, m_old)
    e = jnp.exp2(s * SCALE - m).astype(BF)
    both = jnp.concatenate([vals, jnp.ones_like(vals)], axis=1)
    o = lax.dot_general(both, e, (((0,), (0,)), ((), ())), preferred_element_type=F32)
    return m, o[HEAD : HEAD + 1], o[:HEAD]


def attend_body(n_kv, first, *refs):
    q_ref = refs[0]
    kv_refs = refs[1 : 1 + n_kv]
    if first:
        acc_out, ml_out = refs[1 + n_kv :]
    else:
        acc_in, ml_in, acc_out, ml_out = refs[1 + n_kv :]
    tops = []
    sums = []
    for h in range(GROUP):
        m_old = None if first else ml_in[h : h + 1, :]
        m, l, o = heads_step(q_ref, kv_refs, h, m_old)
        here = slice(h * HEAD, (h + 1) * HEAD)
        if not first:
            alpha = jnp.exp2(m_old - m)
            l = l + alpha * ml_in[8 + h : 9 + h, :]
            o = o + alpha * acc_in[here, :]
        acc_out[here, :] = o
        tops.append(m)
        sums.append(l)
    blank = jnp.zeros((8 - GROUP, QB), F32)
    ml_out[...] = jnp.concatenate([*tops, blank, *sums, blank], axis=0)


def attend(q, kvs, state=None):
    rows = q.shape[0]
    n_keys = sum(kv.shape[0] // 2 for kv in kvs)

    def col(i):
        return (0, i)

    specs = [pl.BlockSpec((QB, GF), lambda i: (i, 0))]
    specs += [pl.BlockSpec(kv.shape, lambda i: (0, 0)) for kv in kvs]
    args = [q, *kvs]
    acc_spec = pl.BlockSpec((GF, QB), col)
    ml_spec = pl.BlockSpec((16, QB), col)
    aliases = {}
    if state is not None:
        aliases = {len(args): 0, len(args) + 1: 1}
        specs += [acc_spec, ml_spec]
        args += list(state)
    return pl.pallas_call(
        lambda *r: attend_body(len(kvs), state is None, *r),
        grid=(rows // QB,),
        in_specs=specs,
        out_specs=[acc_spec, ml_spec],
        out_shape=[
            jax.ShapeDtypeStruct((GF, rows), F32),
            jax.ShapeDtypeStruct((16, rows), F32),
        ],
        input_output_aliases=aliases,
        compiler_params=params(),
        cost_estimate=pl.CostEstimate(
            flops=4 * rows * n_keys * GF,
            transcendentals=rows * n_keys * GROUP,
            bytes_accessed=rows * GF * 10,
        ),
        name="attend",
    )(*args)


def attend_last_body(n_kv, n_out, *refs):
    q_ref = refs[0]
    kv_refs = refs[1 : 1 + n_kv]
    acc_in, ml_in = refs[1 + n_kv : 3 + n_kv]
    outs = refs[3 + n_kv :]
    his, mids, lows = [], [], []
    parts = []
    for h in range(GROUP):
        m_old = ml_in[h : h + 1, :]
        m, l, o = heads_step(q_ref, kv_refs, h, m_old)
        here = slice(h * HEAD, (h + 1) * HEAD)
        alpha = jnp.exp2(m_old - m)
        l = l + alpha * ml_in[8 + h : 9 + h, :]
        o = o + alpha * acc_in[here, :]
        parts.append((o / l).astype(BF))
        lse = m + jnp.log2(l)
        hi = lse.astype(BF).astype(F32)
        mid = (lse - hi).astype(BF).astype(F32)
        his.append(hi)
        mids.append(mid)
        lows.append(lse - hi - mid)
    stats = jnp.concatenate([*his, *mids, *lows, jnp.zeros((1, QB), F32)], axis=0).astype(BF)
    for i in range(n_out):

        @pl.when(pl.program_id(0) == i)
        def _(i=i):
            for h in range(GROUP):
                outs[i][h * HEAD : (h + 1) * HEAD, :] = parts[h]
            outs[i][GF:, :] = stats


def attend_last(q, kvs, state, blocks):
    def place(i):
        back = blocks[0]
        for n, r in enumerate(blocks[1:], 1):
            back = jnp.where(i == n, r, back)
        return back

    n = len(blocks)
    n_keys = sum(kv.shape[0] // 2 for kv in kvs)
    specs = [pl.BlockSpec((QB, GF), lambda i: (place(i), 0))]
    specs += [pl.BlockSpec(kv.shape, lambda i: (0, 0)) for kv in kvs]
    specs += [
        pl.BlockSpec((GF, QB), lambda i: (0, place(i))),
        pl.BlockSpec((16, QB), lambda i: (0, place(i))),
    ]
    return pl.pallas_call(
        lambda *r: attend_last_body(len(kvs), n, *r),
        grid=(n,),
        in_specs=specs,
        out_specs=[pl.BlockSpec((OH, QB), lambda i: (0, 0))] * n,
        out_shape=[jax.ShapeDtypeStruct((OH, QB), BF)] * n,
        compiler_params=params(),
        cost_estimate=pl.CostEstimate(
            flops=4 * n * QB * n_keys * GF,
            transcendentals=n * QB * n_keys * GROUP,
            bytes_accessed=n * QB * GF * 8,
        ),
        name="attend_last",
    )(q, *kvs, *state)


def join_body(*refs):
    parts, out_ref = refs[:-1], refs[-1]
    tails = [p[GF:, :].astype(F32) for p in parts]
    for h in range(GROUP):
        here = slice(h * HEAD, (h + 1) * HEAD)
        lse = [t[h : h + 1] + t[GROUP + h : GROUP + h + 1] + t[2 * GROUP + h : 2 * GROUP + h + 1] for t in tails]
        top = lse[0]
        for other in lse[1:]:
            top = jnp.maximum(top, other)
        weights = [jnp.exp2(v - top) for v in lse]
        total = weights[0]
        for other in weights[1:]:
            total = total + other
        o = weights[0] * parts[0][here, :].astype(F32)
        for w, p in zip(weights[1:], parts[1:]):
            o = o + w * p[here, :].astype(F32)
        out_ref[:, here] = (o / total).T.astype(BF)


def join(parts):
    return pl.pallas_call(
        join_body,
        grid=(2,),
        in_specs=[pl.BlockSpec((OH, QB // 2), lambda i: (0, i))] * len(parts),
        out_specs=pl.BlockSpec((QB // 2, GF), lambda i: (i, 0)),
        out_shape=jax.ShapeDtypeStruct((QB, GF), BF),
        compiler_params=params(),
        name="join",
    )(*parts)


def project_body(blocks, c_ref, own_ref, other_ref, w_ref, *outs):
    lhs = jnp.concatenate(
        [ref[s * ROWS : (s + 1) * ROWS] for s in blocks for ref in (own_ref, other_ref)], axis=0
    )
    y = jnp.dot(lhs, w_ref[...], preferred_element_type=F32).astype(BF)
    for half in range(2):

        @pl.when(pl.program_id(0) == half)
        def _(half=half):
            for i in range(len(blocks)):
                outs[2 * i + half][...] = y[2 * ROWS * i : 2 * ROWS * (i + 1)]


def project(c, own, other, weight, blocks):
    n = 2 * len(blocks)
    grid_spec = pltpu.PrefetchScalarGridSpec(
        num_scalar_prefetch=1,
        grid=(2,),
        in_specs=[
            pl.BlockSpec((QB, GF), lambda i, c_ref: (0, 0)),
            pl.BlockSpec((QB, GF), lambda i, c_ref: (0, 0)),
            pl.BlockSpec((GF, QUART), lambda i, c_ref: (0, c_ref[0] * 2 + i)),
        ],
        out_specs=[pl.BlockSpec((2 * ROWS, QUART), lambda i, c_ref: (0, 0))] * n,
    )
    return pl.pallas_call(
        lambda *r: project_body(blocks, *r),
        grid_spec=grid_spec,
        out_shape=[jax.ShapeDtypeStruct((2 * ROWS, QUART), BF)] * n,
        compiler_params=params(),
        name="project",
    )(c, own, other, weight)


def finish_body(c_ref, own_ref, other_ref, gate_ref, bias_ref, *refs):
    out_ref = refs[-1]
    c = c_ref[0]

    def write(parts):
        mixed = parts[0][...].astype(F32)
        for ref in parts[1:]:
            mixed = mixed + ref[...].astype(F32)
        at = pl.ds(pl.multiple_of((2 * c + pl.program_id(0)) * QUART, HEAD), QUART)
        branch = gate_ref[at][None] * (mixed + bias_ref[at][None])
        out_ref[c] = (own_ref[0].astype(F32) + branch[0:ROWS]).astype(BF)
        out_ref[1 - c] = (other_ref[...].astype(F32) + branch[ROWS:]).astype(BF)

    for half in range(2):

        @pl.when(pl.program_id(0) == half)
        def _(half=half):
            write(refs[half:6:2])


def finish(c, residual, other, gate, bias, parts):
    piece = pl.BlockSpec((2 * ROWS, QUART), lambda i, c_ref: (0, 0))
    line = pl.BlockSpec((D,), lambda i, c_ref: (0,))
    grid_spec = pltpu.PrefetchScalarGridSpec(
        num_scalar_prefetch=1,
        grid=(2,),
        in_specs=[
            pl.BlockSpec((1, ROWS, QUART), lambda i, c_ref: (0, 0, 2 * c_ref[0] + i)),
            pl.BlockSpec((ROWS, QUART), lambda i, c_ref: (0, i)),
            line,
            line,
        ]
        + [piece] * 6,
        out_specs=pl.BlockSpec((2, ROWS, QUART), lambda i, c_ref: (0, 0, i)),
    )
    return pl.pallas_call(
        finish_body,
        grid_spec=grid_spec,
        out_shape=jax.ShapeDtypeStruct((2, ROWS, HALF), BF),
        compiler_params=params(),
        name="finish",
    )(c, residual, other, gate, bias, *parts)


def add(a, b):
    return (a.astype(F32) + b.astype(F32)).astype(BF)


def after(values, *earlier):
    tied = lax.optimization_barrier((tuple(values), earlier))
    return list(tied[0])


def on_device(residual_in, projected, query_gain, key_gain, gate_scale, out_weight, out_bias):
    u = lax.axis_index("uly")
    x = lax.axis_index("x")
    c_arr = lax.axis_index("cfg").astype(jnp.int32)[None]
    first = ((u * XS + x) * ZS + lax.axis_index("z")) * ROWS
    place = jnp.stack([u, first]).astype(jnp.int32)
    sent = prep(place, projected, query_gain, key_gain)

    far = swap_uly(sent[2], 2)
    got = [sent[0], swap_uly(sent[1], 1), far, swap_uly(sent[3], 3)]
    own = jnp.concatenate([a[:ROWS] for a in got] + [a[ROWS : 2 * ROWS] for a in got], axis=0)
    q_own = jnp.concatenate([a[2 * ROWS :] for a in got], axis=0)

    left, right = swap_z(own, 0), swap_z(own, 1)

    (q_sent,) = after([q_own], left)
    q_far = swap_x(q_sent, 2)
    q_all = jnp.concatenate([q_own, swap_x(q_sent, 1), q_far, swap_x(q_sent, 3)], axis=0)

    left2, right2 = swap_z(right, 0), swap_z(left, 1)
    left3, right3 = swap_z(right2, 0), swap_z(left2, 1)
    state = attend(q_all, [own])
    state = attend(q_all, [left, right], state)
    state = attend(q_all, [left2, right2], state)
    left3, right3 = after([left3, right3], *state)
    half = own.shape[0] // 2
    top = jnp.concatenate([right3[: half // 2], right3[half : half + half // 2]], axis=0)
    low = jnp.concatenate([left3[half // 2 : half], left3[half + half // 2 :]], axis=0)
    kvs = [swap_z(top, 0), swap_z(low, 1)]
    state = attend(q_all, [left3, right3], state)

    (p2,) = attend_last(q_all, kvs, state, (2,))
    r2 = swap_x(p2, 2)
    (kv_a,) = after([kvs[0]], p2)
    p1, p3 = attend_last(q_all, [kv_a, kvs[1]], state, (1, 3))
    r1, r3 = swap_x(p1, 1), swap_x(p3, 3)
    (kv_b,) = after([kvs[0]], p1)
    (p0,) = attend_last(q_all, [kv_b, kvs[1]], state, (0,))
    mine = join([p0, r1, r2, r3])
    heads = (mine, swap_cfg(mine))

    p2a, p2b, p1a, p1b, p3a, p3b, p0a, p0b = project(c_arr, *heads, out_weight, (2, 1, 3, 0))
    via_one = swap_uly(p2a, 1)
    via_three = swap_uly(p2b, 3)
    residual_sent = lax.dynamic_slice(residual_in, (0, 0, (1 - c_arr[0]) * HALF), (1, ROWS, HALF))[0]
    (residual_sent,) = after([residual_sent], p1a)
    residual_other = swap_cfg(residual_sent)
    three_b = swap_uly(p3b, 3)
    one_a = swap_uly(p1a, 1)
    three_a = swap_uly(add(p3a, via_one), 3)
    one_b = swap_uly(add(p1b, via_three), 1)
    return finish(
        c_arr,
        residual_in,
        residual_other,
        gate_scale,
        out_bias,
        [p0a, p0b, three_a, three_b, one_a, one_b],
    )


def solution(mesh):
    fine = Mesh(mesh.devices.reshape(2, ULY, XS, ZS), ("cfg", "uly", "x", "z"))
    tokens = ("uly", "x", "z")
    in_specs = (
        P("cfg", tokens, None),
        P("cfg", tokens, None),
        P(),
        P(),
        P(),
        P("uly", None),
        P(),
    )
    out_specs = P(None, tokens, "cfg")
    return jax.shard_map(
        on_device, mesh=fine, in_specs=in_specs, out_specs=out_specs, check_vma=False
    )
```

```python
import math

import jax
import jax.numpy as jnp
import numpy as np
from jax import lax
from jax.experimental import pallas as pl
from jax.experimental.pallas import tpu as pltpu
from jax.sharding import Mesh
from jax.sharding import PartitionSpec as P

D = 5120
HEADS = 20
HEAD = 128
GH = 30
GW = 52
ULY = 4
XS = 4
ZS = 8
ROWS = 64
GROUP = 5
GF = GROUP * HEAD
FEAT = HEADS * HEAD
HALF = D // 2
QUART = HALF // 2
OH = GF + 16
BF = jnp.bfloat16
F32 = jnp.float32
SCALE = math.log2(math.e) / math.sqrt(HEAD)
VMEM = 36 * 1024 * 1024


def params(limit=VMEM):
    return pltpu.CompilerParams(vmem_limit_bytes=limit)


def swap_uly(a, s):
    return lax.ppermute(a, "uly", [(i, i ^ s) for i in range(ULY)])


def swap_x(a, s):
    return lax.ppermute(a, "x", [(i, i ^ s) for i in range(XS)])


def swap_z(a, odd):
    return lax.ppermute(a, "z", [(i, ((i - odd ^ 1) + odd) % ZS) for i in range(ZS)])


def swap_cfg(a):
    return lax.ppermute(a, "cfg", [(0, 1), (1, 0)])


FRAME = HEAD - 4 * (HEAD // 6)
SPACE = 2 * (HEAD // 6)


def rates():
    def freq(extent):
        return 1.0 / 10000.0 ** (np.arange(0, extent, 2, dtype=np.float32) / np.float32(extent))

    each = np.concatenate([freq(FRAME), freq(SPACE), freq(SPACE)]).astype(np.float32)
    return np.repeat(each, 2)[None]


def tables(first, rate):
    pos = first + lax.broadcasted_iota(jnp.int32, (ROWS, HEAD), 0)
    lane = lax.broadcasted_iota(jnp.int32, (ROWS, HEAD), 1)
    where = jnp.where(
        lane < FRAME, pos // (GH * GW), jnp.where(lane < FRAME + SPACE, pos // GW % GH, pos % GW)
    ).astype(F32)
    angle = where * rate
    sine = jnp.sin(angle)
    even = lane % 2 == 0
    return jnp.cos(angle), jnp.where(even, -sine, 0.0), jnp.where(even, 0.0, sine)


def prep_body(width, at_ref, proj_ref, gain_ref, rate_ref, *outs):
    u = at_ref[0]
    cosine, s_even, s_odd = tables(at_ref[1], rate_ref[...])
    total = jnp.zeros((ROWS, HEAD), F32)
    for h in range(HEADS):
        part = proj_ref[0, :, h * HEAD : (h + 1) * HEAD].astype(F32)
        total = total + part * part
    scale = lax.rsqrt(jnp.sum(total, axis=1, keepdims=True) * (1.0 / FEAT) + 1e-06)

    for s in range(ULY):
        start = (u ^ s) * GF
        for h in range(GROUP):
            at = pl.ds(pl.multiple_of(start + h * HEAD, HEAD), HEAD)
            x = proj_ref[0, :, at].astype(F32)
            x = x * scale * gain_ref[at][None]
            x = x * cosine + pltpu.roll(x, HEAD - 1, 1) * s_even + pltpu.roll(x, 1, 1) * s_odd
            outs[s][0:ROWS, h * HEAD : (h + 1) * HEAD] = x.astype(BF)
        if width == 2:
            outs[s][ROWS:, :] = proj_ref[0, :, pl.ds(pl.multiple_of(FEAT + start, HEAD), GF)]


def prep(place, projected, gain, width):
    def whole(shape):
        return pl.BlockSpec(shape, lambda i: (0,) * len(shape))

    part = pl.BlockSpec(
        (pl.Element(1), pl.Element(ROWS), pl.Element(width * FEAT)),
        lambda i: (0, 0, FEAT * (width - 1)),
    )
    rate = jnp.asarray(rates())
    return pl.pallas_call(
        lambda *r: prep_body(width, *r),
        grid=(1,),
        in_specs=[pl.BlockSpec(memory_space=pltpu.SMEM), part, whole(gain.shape), whole(rate.shape)],
        out_specs=[whole((width * ROWS, GF))] * ULY,
        out_shape=[jax.ShapeDtypeStruct((width * ROWS, GF), BF)] * ULY,
        compiler_params=params(62 * 1024 * 1024),
        cost_estimate=pl.CostEstimate(flops=4000000, transcendentals=20000, bytes_accessed=2000000),
        name="prep",
    )(place, projected, gain, rate)


QB = 256


def heads_step(q, kvs, h, m_old):
    here = slice(h * HEAD, (h + 1) * HEAD)
    keys = jnp.concatenate([kv[0 : kv.shape[0] // 2, here] for kv in kvs], axis=0)
    vals = jnp.concatenate([kv[kv.shape[0] // 2 :, here] for kv in kvs], axis=0)
    s = lax.dot_general(keys, q[:, here], (((1,), (1,)), ((), ())), preferred_element_type=F32)
    m = jnp.max(s, axis=0, keepdims=True) * SCALE
    if m_old is not None:
        m = jnp.maximum(m, m_old)
    e = jnp.exp2(s * SCALE - m).astype(BF)
    both = jnp.concatenate([vals, jnp.ones_like(vals)], axis=1)
    o = lax.dot_general(both, e, (((0,), (0,)), ((), ())), preferred_element_type=F32)
    return m, o[HEAD : HEAD + 1], o[:HEAD]


def attend_body(n_kv, first, *refs):
    q_ref = refs[0]
    kv_refs = refs[1 : 1 + n_kv]
    if first:
        acc_out, ml_out = refs[1 + n_kv :]
    else:
        acc_in, ml_in, acc_out, ml_out = refs[1 + n_kv :]
    tops = []
    sums = []
    for h in range(GROUP):
        m_old = None if first else ml_in[h : h + 1, :]
        m, l, o = heads_step(q_ref, kv_refs, h, m_old)
        here = slice(h * HEAD, (h + 1) * HEAD)
        if not first:
            alpha = jnp.exp2(m_old - m)
            l = l + alpha * ml_in[8 + h : 9 + h, :]
            o = o + alpha * acc_in[here, :]
        acc_out[here, :] = o
        tops.append(m)
        sums.append(l)
    blank = jnp.zeros((8 - GROUP, QB), F32)
    ml_out[...] = jnp.concatenate([*tops, blank, *sums, blank], axis=0)


def attend(q, kvs, state=None):
    rows = q.shape[0]
    n_keys = sum(kv.shape[0] // 2 for kv in kvs)

    def col(i):
        return (0, i)

    specs = [pl.BlockSpec((QB, GF), lambda i: (i, 0))]
    specs += [pl.BlockSpec(kv.shape, lambda i: (0, 0)) for kv in kvs]
    args = [q, *kvs]
    acc_spec = pl.BlockSpec((GF, QB), col)
    ml_spec = pl.BlockSpec((16, QB), col)
    aliases = {}
    if state is not None:
        aliases = {len(args): 0, len(args) + 1: 1}
        specs += [acc_spec, ml_spec]
        args += list(state)
    return pl.pallas_call(
        lambda *r: attend_body(len(kvs), state is None, *r),
        grid=(rows // QB,),
        in_specs=specs,
        out_specs=[acc_spec, ml_spec],
        out_shape=[
            jax.ShapeDtypeStruct((GF, rows), F32),
            jax.ShapeDtypeStruct((16, rows), F32),
        ],
        input_output_aliases=aliases,
        compiler_params=params(),
        cost_estimate=pl.CostEstimate(
            flops=4 * rows * n_keys * GF,
            transcendentals=rows * n_keys * GROUP,
            bytes_accessed=rows * GF * 10,
        ),
        name="attend",
    )(*args)


def attend_last_body(n_kv, n_out, *refs):
    q_ref = refs[0]
    kv_refs = refs[1 : 1 + n_kv]
    acc_in, ml_in = refs[1 + n_kv : 3 + n_kv]
    outs = refs[3 + n_kv :]
    his, mids, lows = [], [], []
    parts = []
    for h in range(GROUP):
        m_old = ml_in[h : h + 1, :]
        m, l, o = heads_step(q_ref, kv_refs, h, m_old)
        here = slice(h * HEAD, (h + 1) * HEAD)
        alpha = jnp.exp2(m_old - m)
        l = l + alpha * ml_in[8 + h : 9 + h, :]
        o = o + alpha * acc_in[here, :]
        parts.append((o / l).astype(BF))
        lse = m + jnp.log2(l)
        hi = lse.astype(BF).astype(F32)
        mid = (lse - hi).astype(BF).astype(F32)
        his.append(hi)
        mids.append(mid)
        lows.append(lse - hi - mid)
    stats = jnp.concatenate([*his, *mids, *lows, jnp.zeros((1, QB), F32)], axis=0).astype(BF)
    for i in range(n_out):

        @pl.when(pl.program_id(0) == i)
        def _(i=i):
            for h in range(GROUP):
                outs[i][h * HEAD : (h + 1) * HEAD, :] = parts[h]
            outs[i][GF:, :] = stats


def attend_last(q, kvs, state, blocks):
    def place(i):
        back = blocks[0]
        for n, r in enumerate(blocks[1:], 1):
            back = jnp.where(i == n, r, back)
        return back

    n = len(blocks)
    n_keys = sum(kv.shape[0] // 2 for kv in kvs)
    specs = [pl.BlockSpec((QB, GF), lambda i: (place(i), 0))]
    specs += [pl.BlockSpec(kv.shape, lambda i: (0, 0)) for kv in kvs]
    specs += [
        pl.BlockSpec((GF, QB), lambda i: (0, place(i))),
        pl.BlockSpec((16, QB), lambda i: (0, place(i))),
    ]
    return pl.pallas_call(
        lambda *r: attend_last_body(len(kvs), n, *r),
        grid=(n,),
        in_specs=specs,
        out_specs=[pl.BlockSpec((OH, QB), lambda i: (0, 0))] * n,
        out_shape=[jax.ShapeDtypeStruct((OH, QB), BF)] * n,
        compiler_params=params(),
        cost_estimate=pl.CostEstimate(
            flops=4 * n * QB * n_keys * GF,
            transcendentals=n * QB * n_keys * GROUP,
            bytes_accessed=n * QB * GF * 8,
        ),
        name="attend_last",
    )(q, *kvs, *state)


def join_body(*refs):
    parts, out_ref = refs[:-1], refs[-1]
    tails = [p[GF:, :].astype(F32) for p in parts]
    for h in range(GROUP):
        here = slice(h * HEAD, (h + 1) * HEAD)
        lse = [t[h : h + 1] + t[GROUP + h : GROUP + h + 1] + t[2 * GROUP + h : 2 * GROUP + h + 1] for t in tails]
        top = lse[0]
        for other in lse[1:]:
            top = jnp.maximum(top, other)
        weights = [jnp.exp2(v - top) for v in lse]
        total = weights[0]
        for other in weights[1:]:
            total = total + other
        o = weights[0] * parts[0][here, :].astype(F32)
        for w, p in zip(weights[1:], parts[1:]):
            o = o + w * p[here, :].astype(F32)
        out_ref[:, here] = (o / total).T.astype(BF)


def join(parts):
    return pl.pallas_call(
        join_body,
        grid=(2,),
        in_specs=[pl.BlockSpec((OH, QB // 2), lambda i: (0, i))] * len(parts),
        out_specs=pl.BlockSpec((QB // 2, GF), lambda i: (i, 0)),
        out_shape=jax.ShapeDtypeStruct((QB, GF), BF),
        compiler_params=params(),
        name="join",
    )(*parts)


def project_body(blocks, c_ref, own_ref, other_ref, w_ref, *outs):
    lhs = jnp.concatenate(
        [ref[s * ROWS : (s + 1) * ROWS] for s in blocks for ref in (own_ref, other_ref)], axis=0
    )
    y = jnp.dot(lhs, w_ref[...], preferred_element_type=F32).astype(BF)
    for half in range(2):

        @pl.when(pl.program_id(0) == half)
        def _(half=half):
            for i in range(len(blocks)):
                outs[2 * i + half][...] = y[2 * ROWS * i : 2 * ROWS * (i + 1)]


def project(c, own, other, weight, blocks):
    n = 2 * len(blocks)
    grid_spec = pltpu.PrefetchScalarGridSpec(
        num_scalar_prefetch=1,
        grid=(2,),
        in_specs=[
            pl.BlockSpec((QB, GF), lambda i, c_ref: (0, 0)),
            pl.BlockSpec((QB, GF), lambda i, c_ref: (0, 0)),
            pl.BlockSpec((GF, QUART), lambda i, c_ref: (0, c_ref[0] * 2 + i)),
        ],
        out_specs=[pl.BlockSpec((2 * ROWS, QUART), lambda i, c_ref: (0, 0))] * n,
    )
    return pl.pallas_call(
        lambda *r: project_body(blocks, *r),
        grid_spec=grid_spec,
        out_shape=[jax.ShapeDtypeStruct((2 * ROWS, QUART), BF)] * n,
        compiler_params=params(),
        name="project",
    )(c, own, other, weight)


def finish_body(c_ref, own_ref, other_ref, gate_ref, bias_ref, *refs):
    out_ref = refs[-1]
    c = c_ref[0]

    def write(parts):
        mixed = parts[0][...].astype(F32)
        for ref in parts[1:]:
            mixed = mixed + ref[...].astype(F32)
        at = pl.ds(pl.multiple_of((2 * c + pl.program_id(0)) * QUART, HEAD), QUART)
        branch = gate_ref[at][None] * (mixed + bias_ref[at][None])
        out_ref[c] = (own_ref[0].astype(F32) + branch[0:ROWS]).astype(BF)
        out_ref[1 - c] = (other_ref[...].astype(F32) + branch[ROWS:]).astype(BF)

    for half in range(2):

        @pl.when(pl.program_id(0) == half)
        def _(half=half):
            write(refs[half:6:2])


def finish(c, residual, other, gate, bias, parts):
    piece = pl.BlockSpec((2 * ROWS, QUART), lambda i, c_ref: (0, 0))
    line = pl.BlockSpec((D,), lambda i, c_ref: (0,))
    grid_spec = pltpu.PrefetchScalarGridSpec(
        num_scalar_prefetch=1,
        grid=(2,),
        in_specs=[
            pl.BlockSpec((1, ROWS, QUART), lambda i, c_ref: (0, 0, 2 * c_ref[0] + i)),
            pl.BlockSpec((ROWS, QUART), lambda i, c_ref: (0, i)),
            line,
            line,
        ]
        + [piece] * 6,
        out_specs=pl.BlockSpec((2, ROWS, QUART), lambda i, c_ref: (0, 0, i)),
    )
    return pl.pallas_call(
        finish_body,
        grid_spec=grid_spec,
        out_shape=jax.ShapeDtypeStruct((2, ROWS, HALF), BF),
        compiler_params=params(),
        name="finish",
    )(c, residual, other, gate, bias, *parts)


def add(a, b):
    return (a.astype(F32) + b.astype(F32)).astype(BF)


def after(values, *earlier):
    tied = lax.optimization_barrier((tuple(values), earlier))
    return list(tied[0])


def on_device(residual_in, projected, query_gain, key_gain, gate_scale, out_weight, out_bias):
    u = lax.axis_index("uly")
    x = lax.axis_index("x")
    c_arr = lax.axis_index("cfg").astype(jnp.int32)[None]
    first = ((u * XS + x) * ZS + lax.axis_index("z")) * ROWS
    place = jnp.stack([u, first]).astype(jnp.int32)
    def by_heads(sent):
        far = swap_uly(sent[2], 2)
        return [sent[0], swap_uly(sent[1], 1), far, swap_uly(sent[3], 3)]

    got = by_heads(prep(place, projected, key_gain, 2))
    own = jnp.concatenate([a[:ROWS] for a in got] + [a[ROWS:] for a in got], axis=0)

    left, right = swap_z(own, 0), swap_z(own, 1)

    (place,) = after([place], own)
    q_own = jnp.concatenate(by_heads(prep(place, projected, query_gain, 1)), axis=0)
    (q_sent,) = after([q_own], left)
    q1, q3 = swap_x(q_sent, 1), swap_x(q_sent, 3)
    q2 = [swap_x(q3[: QB // 2], 1), swap_x(q1[QB // 2 :], 3)]
    q_all = jnp.concatenate([q_own, q1, *q2, q3], axis=0)

    left2, right2 = swap_z(right, 0), swap_z(left, 1)
    state = attend(q_all, [own])
    state = attend(q_all, [left, right], state)
    left3, right3 = swap_z(right2, 0), swap_z(left2, 1)
    state = attend(q_all, [left2, right2], state)
    left3, right3 = after([left3, right3], *state)
    half = own.shape[0] // 2
    top = jnp.concatenate([right3[: half // 2], right3[half : half + half // 2]], axis=0)
    low = jnp.concatenate([left3[half // 2 : half], left3[half + half // 2 :]], axis=0)
    kvs = [swap_z(top, 0), swap_z(low, 1)]
    state = attend(q_all, [left3, right3], state)

    residual_sent = lax.dynamic_slice(residual_in, (0, 0, (1 - c_arr[0]) * HALF), (1, ROWS, HALF))[0]
    (residual_sent,) = after([residual_sent], left2)
    residual_other = swap_cfg(residual_sent)

    (p2,) = attend_last(q_all, kvs, state, (2,))
    r2 = swap_x(p2, 2)
    (kv_a,) = after([kvs[0]], p2)
    p1, p3 = attend_last(q_all, [kv_a, kvs[1]], state, (1, 3))
    r1, r3 = swap_x(p1, 1), swap_x(p3, 3)
    (kv_b,) = after([kvs[0]], p1)
    (p0,) = attend_last(q_all, [kv_b, kvs[1]], state, (0,))
    mine = join([p0, r1, r2, r3])
    (mine,) = after([mine], residual_other)
    heads = (mine, swap_cfg(mine))

    p2a, p2b = project(c_arr, *heads, out_weight, (2,))
    via_one = swap_uly(p2a, 1)
    via_three = swap_uly(p2b, 3)
    p1a, p1b, p3a, p3b, p0a, p0b = project(c_arr, *heads, out_weight, (1, 3, 0))
    three_b = swap_uly(p3b, 3)
    one_a = swap_uly(p1a, 1)
    three_a = swap_uly(add(p3a, via_one), 3)
    one_b = swap_uly(add(p1b, via_three), 1)
    return finish(
        c_arr,
        residual_in,
        residual_other,
        gate_scale,
        out_bias,
        [p0a, p0b, three_a, three_b, one_a, one_b],
    )


def solution(mesh):
    fine = Mesh(mesh.devices.reshape(2, ULY, XS, ZS), ("cfg", "uly", "x", "z"))
    tokens = ("uly", "x", "z")
    in_specs = (
        P("cfg", tokens, None),
        P("cfg", tokens, None),
        P(),
        P(),
        P(),
        P("uly", None),
        P(),
    )
    out_specs = P(None, tokens, "cfg")
    return jax.shard_map(
        on_device, mesh=fine, in_specs=in_specs, out_specs=out_specs, check_vma=False
    )
```

```python
import math

import jax
import jax.numpy as jnp
import numpy as np
from jax import lax
from jax.experimental import pallas as pl
from jax.experimental.pallas import tpu as pltpu
from jax.sharding import Mesh
from jax.sharding import PartitionSpec as P

D = 5120
HEADS = 20
HEAD = 128
GH = 30
GW = 52
ULY = 4
XS = 4
ZS = 8
ROWS = 64
GROUP = 5
GF = GROUP * HEAD
FEAT = HEADS * HEAD
HALF = D // 2
QUART = HALF // 2
OH = GF + 16
BF = jnp.bfloat16
F32 = jnp.float32
SCALE = math.log2(math.e) / math.sqrt(HEAD)
VMEM = 36 * 1024 * 1024


def params(limit=VMEM):
    return pltpu.CompilerParams(vmem_limit_bytes=limit)


def swap_uly(a, s):
    return lax.ppermute(a, "uly", [(i, i ^ s) for i in range(ULY)])


def swap_x(a, s):
    return lax.ppermute(a, "x", [(i, i ^ s) for i in range(XS)])


def swap_z(a, odd):
    return lax.ppermute(a, "z", [(i, ((i - odd ^ 1) + odd) % ZS) for i in range(ZS)])


def swap_cfg(a):
    return lax.ppermute(a, "cfg", [(0, 1), (1, 0)])


FRAME = HEAD - 4 * (HEAD // 6)
SPACE = 2 * (HEAD // 6)


def rates():
    def freq(extent):
        return 1.0 / 10000.0 ** (np.arange(0, extent, 2, dtype=np.float32) / np.float32(extent))

    each = np.concatenate([freq(FRAME), freq(SPACE), freq(SPACE)]).astype(np.float32)
    return np.repeat(each, 2)[None]


def tables(first, rate):
    pos = first + lax.broadcasted_iota(jnp.int32, (ROWS, HEAD), 0)
    lane = lax.broadcasted_iota(jnp.int32, (ROWS, HEAD), 1)
    where = jnp.where(
        lane < FRAME, pos // (GH * GW), jnp.where(lane < FRAME + SPACE, pos // GW % GH, pos % GW)
    ).astype(F32)
    angle = where * rate
    sine = jnp.sin(angle)
    even = lane % 2 == 0
    return jnp.cos(angle), jnp.where(even, -sine, 0.0), jnp.where(even, 0.0, sine)


def prep_body(width, at_ref, proj_ref, gain_ref, rate_ref, *outs):
    u = at_ref[0]
    cosine, s_even, s_odd = tables(at_ref[1], rate_ref[...])
    total = jnp.zeros((ROWS, HEAD), F32)
    for h in range(HEADS):
        part = proj_ref[0, :, h * HEAD : (h + 1) * HEAD].astype(F32)
        total = total + part * part
    scale = lax.rsqrt(jnp.sum(total, axis=1, keepdims=True) * (1.0 / FEAT) + 1e-06)

    for s in range(ULY):
        start = (u ^ s) * GF
        for h in range(GROUP):
            at = pl.ds(pl.multiple_of(start + h * HEAD, HEAD), HEAD)
            x = proj_ref[0, :, at].astype(F32)
            x = x * scale * gain_ref[at][None]
            x = x * cosine + pltpu.roll(x, HEAD - 1, 1) * s_even + pltpu.roll(x, 1, 1) * s_odd
            outs[s][0:ROWS, h * HEAD : (h + 1) * HEAD] = x.astype(BF)
        if width == 2:
            outs[s][ROWS:, :] = proj_ref[0, :, pl.ds(pl.multiple_of(FEAT + start, HEAD), GF)]


def prep(place, projected, gain, width):
    def whole(shape):
        return pl.BlockSpec(shape, lambda i: (0,) * len(shape))

    part = pl.BlockSpec(
        (pl.Element(1), pl.Element(ROWS), pl.Element(width * FEAT)),
        lambda i: (0, 0, FEAT * (width - 1)),
    )
    rate = jnp.asarray(rates())
    return pl.pallas_call(
        lambda *r: prep_body(width, *r),
        grid=(1,),
        in_specs=[pl.BlockSpec(memory_space=pltpu.SMEM), part, whole(gain.shape), whole(rate.shape)],
        out_specs=[whole((width * ROWS, GF))] * ULY,
        out_shape=[jax.ShapeDtypeStruct((width * ROWS, GF), BF)] * ULY,
        compiler_params=params(62 * 1024 * 1024),
        cost_estimate=pl.CostEstimate(flops=4000000, transcendentals=20000, bytes_accessed=2000000),
        name="prep",
    )(place, projected, gain, rate)


QB = 256


def heads_step(q, kvs, h, m_old, apart=False):
    here = slice(h * HEAD, (h + 1) * HEAD)
    if apart:
        keys, vals = (kv[:, here] for kv in kvs)
    else:
        keys = jnp.concatenate([kv[0 : kv.shape[0] // 2, here] for kv in kvs], axis=0)
        vals = jnp.concatenate([kv[kv.shape[0] // 2 :, here] for kv in kvs], axis=0)
    s = lax.dot_general(keys, q[:, here], (((1,), (1,)), ((), ())), preferred_element_type=F32)
    m = jnp.max(s, axis=0, keepdims=True) * SCALE
    if m_old is not None:
        m = jnp.maximum(m, m_old)
    e = jnp.exp2(s * SCALE - m).astype(BF)
    both = jnp.concatenate([vals, jnp.ones_like(vals)], axis=1)
    o = lax.dot_general(both, e, (((0,), (0,)), ((), ())), preferred_element_type=F32)
    return m, o[HEAD : HEAD + 1], o[:HEAD]


def attend_body(n_kv, first, *refs):
    q_ref = refs[0]
    kv_refs = refs[1 : 1 + n_kv]
    if first:
        acc_out, ml_out = refs[1 + n_kv :]
    else:
        acc_in, ml_in, acc_out, ml_out = refs[1 + n_kv :]
    tops = []
    sums = []
    for h in range(GROUP):
        m_old = None if first else ml_in[h : h + 1, :]
        m, l, o = heads_step(q_ref, kv_refs, h, m_old)
        here = slice(h * HEAD, (h + 1) * HEAD)
        if not first:
            alpha = jnp.exp2(m_old - m)
            l = l + alpha * ml_in[8 + h : 9 + h, :]
            o = o + alpha * acc_in[here, :]
        acc_out[here, :] = o
        tops.append(m)
        sums.append(l)
    blank = jnp.zeros((8 - GROUP, QB), F32)
    ml_out[...] = jnp.concatenate([*tops, blank, *sums, blank], axis=0)


def attend(q, kvs, state=None):
    rows = q.shape[0]
    n_keys = sum(kv.shape[0] // 2 for kv in kvs)

    def col(i):
        return (0, i)

    specs = [pl.BlockSpec((QB, GF), lambda i: (i, 0))]
    specs += [pl.BlockSpec(kv.shape, lambda i: (0, 0)) for kv in kvs]
    args = [q, *kvs]
    acc_spec = pl.BlockSpec((GF, QB), col)
    ml_spec = pl.BlockSpec((16, QB), col)
    aliases = {}
    if state is not None:
        aliases = {len(args): 0, len(args) + 1: 1}
        specs += [acc_spec, ml_spec]
        args += list(state)
    return pl.pallas_call(
        lambda *r: attend_body(len(kvs), state is None, *r),
        grid=(rows // QB,),
        in_specs=specs,
        out_specs=[acc_spec, ml_spec],
        out_shape=[
            jax.ShapeDtypeStruct((GF, rows), F32),
            jax.ShapeDtypeStruct((16, rows), F32),
        ],
        input_output_aliases=aliases,
        compiler_params=params(),
        cost_estimate=pl.CostEstimate(
            flops=4 * rows * n_keys * GF,
            transcendentals=rows * n_keys * GROUP,
            bytes_accessed=rows * GF * 10,
        ),
        name="attend",
    )(*args)


def attend_last_body(n_kv, n_out, *refs):
    q_ref = refs[0]
    kv_refs = refs[1 : 1 + n_kv]
    acc_in, ml_in = refs[1 + n_kv : 3 + n_kv]
    outs = refs[3 + n_kv :]
    his, mids, lows = [], [], []
    parts = []
    for h in range(GROUP):
        m_old = ml_in[h : h + 1, :]
        m, l, o = heads_step(q_ref, kv_refs, h, m_old, True)
        here = slice(h * HEAD, (h + 1) * HEAD)
        alpha = jnp.exp2(m_old - m)
        l = l + alpha * ml_in[8 + h : 9 + h, :]
        o = o + alpha * acc_in[here, :]
        parts.append((o / l).astype(BF))
        lse = m + jnp.log2(l)
        hi = lse.astype(BF).astype(F32)
        mid = (lse - hi).astype(BF).astype(F32)
        his.append(hi)
        mids.append(mid)
        lows.append(lse - hi - mid)
    stats = jnp.concatenate([*his, *mids, *lows, jnp.zeros((1, QB), F32)], axis=0).astype(BF)
    for i in range(n_out):

        @pl.when(pl.program_id(0) == i)
        def _(i=i):
            for h in range(GROUP):
                outs[i][h * HEAD : (h + 1) * HEAD, :] = parts[h]
            outs[i][GF:, :] = stats


def attend_last(q, kvs, state, blocks):
    def place(i):
        back = blocks[0]
        for n, r in enumerate(blocks[1:], 1):
            back = jnp.where(i == n, r, back)
        return back

    n = len(blocks)
    n_keys = sum(kv.shape[0] // 2 for kv in kvs)
    specs = [pl.BlockSpec((QB, GF), lambda i: (place(i), 0))]
    specs += [pl.BlockSpec(kv.shape, lambda i: (0, 0)) for kv in kvs]
    specs += [
        pl.BlockSpec((GF, QB), lambda i: (0, place(i))),
        pl.BlockSpec((16, QB), lambda i: (0, place(i))),
    ]
    return pl.pallas_call(
        lambda *r: attend_last_body(len(kvs), n, *r),
        grid=(n,),
        in_specs=specs,
        out_specs=[pl.BlockSpec((OH, QB), lambda i: (0, 0))] * n,
        out_shape=[jax.ShapeDtypeStruct((OH, QB), BF)] * n,
        compiler_params=params(),
        cost_estimate=pl.CostEstimate(
            flops=4 * n * QB * n_keys * GF,
            transcendentals=n * QB * n_keys * GROUP,
            bytes_accessed=n * QB * GF * 8,
        ),
        name="attend_last",
    )(q, *kvs, *state)


def join_body(*refs):
    parts, out_ref = refs[:-1], refs[-1]
    tails = [p[GF:, :].astype(F32) for p in parts]
    for h in range(GROUP):
        here = slice(h * HEAD, (h + 1) * HEAD)
        lse = [t[h : h + 1] + t[GROUP + h : GROUP + h + 1] + t[2 * GROUP + h : 2 * GROUP + h + 1] for t in tails]
        top = lse[0]
        for other in lse[1:]:
            top = jnp.maximum(top, other)
        weights = [jnp.exp2(v - top) for v in lse]
        total = weights[0]
        for other in weights[1:]:
            total = total + other
        o = weights[0] * parts[0][here, :].astype(F32)
        for w, p in zip(weights[1:], parts[1:]):
            o = o + w * p[here, :].astype(F32)
        out_ref[:, here] = (o / total).T.astype(BF)


def join(parts):
    return pl.pallas_call(
        join_body,
        grid=(2,),
        in_specs=[pl.BlockSpec((OH, QB // 2), lambda i: (0, i))] * len(parts),
        out_specs=pl.BlockSpec((QB // 2, GF), lambda i: (i, 0)),
        out_shape=jax.ShapeDtypeStruct((QB, GF), BF),
        compiler_params=params(),
        name="join",
    )(*parts)


def project_body(blocks, c_ref, own_ref, other_ref, w_ref, *outs):
    lhs = jnp.concatenate(
        [ref[s * ROWS : (s + 1) * ROWS] for s in blocks for ref in (own_ref, other_ref)], axis=0
    )
    y = jnp.dot(lhs, w_ref[...], preferred_element_type=F32).astype(BF)
    for half in range(2):

        @pl.when(pl.program_id(0) == half)
        def _(half=half):
            for i in range(len(blocks)):
                outs[2 * i + half][...] = y[2 * ROWS * i : 2 * ROWS * (i + 1)]


def project(c, own, other, weight, blocks):
    n = 2 * len(blocks)
    grid_spec = pltpu.PrefetchScalarGridSpec(
        num_scalar_prefetch=1,
        grid=(2,),
        in_specs=[
            pl.BlockSpec((QB, GF), lambda i, c_ref: (0, 0)),
            pl.BlockSpec((QB, GF), lambda i, c_ref: (0, 0)),
            pl.BlockSpec((GF, QUART), lambda i, c_ref: (0, c_ref[0] * 2 + i)),
        ],
        out_specs=[pl.BlockSpec((2 * ROWS, QUART), lambda i, c_ref: (0, 0))] * n,
    )
    return pl.pallas_call(
        lambda *r: project_body(blocks, *r),
        grid_spec=grid_spec,
        out_shape=[jax.ShapeDtypeStruct((2 * ROWS, QUART), BF)] * n,
        compiler_params=params(),
        name="project",
    )(c, own, other, weight)


def finish_body(c_ref, own_ref, other_ref, gate_ref, bias_ref, *refs):
    out_ref = refs[-1]
    c = c_ref[0]

    def write(parts):
        mixed = parts[0][...].astype(F32)
        for ref in parts[1:]:
            mixed = mixed + ref[...].astype(F32)
        at = pl.ds(pl.multiple_of((2 * c + pl.program_id(0)) * QUART, HEAD), QUART)
        branch = gate_ref[at][None] * (mixed + bias_ref[at][None])
        out_ref[c] = (own_ref[0].astype(F32) + branch[0:ROWS]).astype(BF)
        out_ref[1 - c] = (other_ref[...].astype(F32) + branch[ROWS:]).astype(BF)

    for half in range(2):

        @pl.when(pl.program_id(0) == half)
        def _(half=half):
            write(refs[half:6:2])


def finish(c, residual, other, gate, bias, parts):
    piece = pl.BlockSpec((2 * ROWS, QUART), lambda i, c_ref: (0, 0))
    line = pl.BlockSpec((D,), lambda i, c_ref: (0,))
    grid_spec = pltpu.PrefetchScalarGridSpec(
        num_scalar_prefetch=1,
        grid=(2,),
        in_specs=[
            pl.BlockSpec((1, ROWS, QUART), lambda i, c_ref: (0, 0, 2 * c_ref[0] + i)),
            pl.BlockSpec((ROWS, QUART), lambda i, c_ref: (0, i)),
            line,
            line,
        ]
        + [piece] * 6,
        out_specs=pl.BlockSpec((2, ROWS, QUART), lambda i, c_ref: (0, 0, i)),
    )
    return pl.pallas_call(
        finish_body,
        grid_spec=grid_spec,
        out_shape=jax.ShapeDtypeStruct((2, ROWS, HALF), BF),
        compiler_params=params(),
        name="finish",
    )(c, residual, other, gate, bias, *parts)


def add(a, b):
    return (a.astype(F32) + b.astype(F32)).astype(BF)


def after(values, *earlier):
    tied = lax.optimization_barrier((tuple(values), earlier))
    return list(tied[0])


def on_device(residual_in, projected, query_gain, key_gain, gate_scale, out_weight, out_bias):
    u = lax.axis_index("uly")
    x = lax.axis_index("x")
    c_arr = lax.axis_index("cfg").astype(jnp.int32)[None]
    first = ((u * XS + x) * ZS + lax.axis_index("z")) * ROWS
    place = jnp.stack([u, first]).astype(jnp.int32)
    def by_heads(sent):
        far = swap_uly(sent[2], 2)
        return [sent[0], swap_uly(sent[1], 1), far, swap_uly(sent[3], 3)]

    got = by_heads(prep(place, projected, key_gain, 2))
    own = jnp.concatenate([a[:ROWS] for a in got] + [a[ROWS:] for a in got], axis=0)

    left, right = swap_z(own, 0), swap_z(own, 1)

    (place,) = after([place], own)
    q_own = jnp.concatenate(by_heads(prep(place, projected, query_gain, 1)), axis=0)
    (q_sent,) = after([q_own], left)
    q1, q3 = swap_x(q_sent, 1), swap_x(q_sent, 3)
    q2 = [swap_x(q3[: QB // 2], 1), swap_x(q1[QB // 2 :], 3)]
    q_all = jnp.concatenate([q_own, q1, *q2, q3], axis=0)

    left2, right2 = swap_z(right, 0), swap_z(left, 1)
    state = attend(q_all, [own])
    state = attend(q_all, [left, right], state)
    left3, right3 = swap_z(right2, 0), swap_z(left2, 1)
    state = attend(q_all, [left2, right2], state)
    half = own.shape[0] // 2
    top, low = after([right3[:half], left3[half:]], *state)
    kvs = [swap_z(top, 0), swap_z(low, 1)]
    state = attend(q_all, [left3, right3], state)

    residual_sent = lax.dynamic_slice(residual_in, (0, 0, (1 - c_arr[0]) * HALF), (1, ROWS, HALF))[0]
    (residual_sent,) = after([residual_sent], left2)
    residual_other = swap_cfg(residual_sent)

    (p2,) = attend_last(q_all, kvs, state, (2,))
    r2 = swap_x(p2, 2)
    (kv_a,) = after([kvs[0]], p2)
    p1, p3 = attend_last(q_all, [kv_a, kvs[1]], state, (1, 3))
    r1, r3 = swap_x(p1, 1), swap_x(p3, 3)
    (kv_b,) = after([kvs[0]], p1)
    (p0,) = attend_last(q_all, [kv_b, kvs[1]], state, (0,))
    mine = join([p0, r1, r2, r3])
    (mine,) = after([mine], residual_other)
    heads = (mine, swap_cfg(mine))

    p2a, p2b = project(c_arr, *heads, out_weight, (2,))
    via_one = swap_uly(p2a, 1)
    via_three = swap_uly(p2b, 3)
    p1a, p1b, p3a, p3b, p0a, p0b = project(c_arr, *heads, out_weight, (1, 3, 0))
    three_b = swap_uly(p3b, 3)
    one_a = swap_uly(p1a, 1)
    three_a = swap_uly(add(p3a, via_one), 3)
    one_b = swap_uly(add(p1b, via_three), 1)
    return finish(
        c_arr,
        residual_in,
        residual_other,
        gate_scale,
        out_bias,
        [p0a, p0b, three_a, three_b, one_a, one_b],
    )


def solution(mesh):
    fine = Mesh(mesh.devices.reshape(2, ULY, XS, ZS), ("cfg", "uly", "x", "z"))
    tokens = ("uly", "x", "z")
    in_specs = (
        P("cfg", tokens, None),
        P("cfg", tokens, None),
        P(),
        P(),
        P(),
        P("uly", None),
        P(),
    )
    out_specs = P(None, tokens, "cfg")
    return jax.shard_map(
        on_device, mesh=fine, in_specs=in_specs, out_specs=out_specs, check_vma=False
    )
```
